32 devices in a mesh: dp: 16 (over z, y, x), mp: 2 (over core).
Axes of the slice: x: 2, y: 2, z: 4, core: 2. Of those that a mesh axis runs over, the one named last changes fastest.
Arguments:
- frames: bfloat16 [8192, 768], P(('dp', 'mp')), may hold values from -6 to 6
- qkv_weight: bfloat16 [2, 768, 3, 768], P(None, None, None, 'mp'), may hold values from -0.21875 to 0.21875
- qv_bias: float32 [2, 2, 768], P(None, None, 'mp'), may hold values from -1.75 to 1.75
- out_weight: bfloat16 [2, 768, 768], P(None, 'mp'), may hold values from -0.875 to 0.875
- up_weight: bfloat16 [2, 768, 3072], P(None, None, 'mp'), may hold values from -0.21875 to 0.21875
- up_bias: float32 [2, 3072], P(None, 'mp'), may hold values from -3 to 3
- down_weight: bfloat16 [2, 3072, 768], P(None, 'mp'), may hold values from -0.15625 to 0.15625
- out_bias: float32 [2, 2, 768], replicated, may hold values from -1.75 to 1.75
- norm_gain: float32 [2, 2, 768], replicated, may hold values from 0.25 to 1.75
- norm_shift: float32 [2, 2, 768], replicated, may hold values from -1.75 to 1.75
- clip_lengths: int32 [128], P('dp'), may hold values from 0 to 512, as said below
- live_lengths: int32 [128], P('dp'), may hold values from 0 to 512, as said below
- out_grad: bfloat16 [8192, 768], P(('dp', 'mp')), may hold values from -12 to 12
Outputs:
- frames_out: bfloat16 [8192, 768], P(('dp', 'mp'))
- input_grad: float32 [8192, 768], P(('dp', 'mp'))
- qkv_weight_grad: float32 [2, 768, 3, 768], P(None, 'dp', None, 'mp')
- qv_bias_grad: float32 [2, 2, 2, 384], P(None, 'mp', None, 'dp')
- out_weight_grad: float32 [2, 768, 768], P(None, 'mp', 'dp')
- up_weight_grad: float32 [2, 768, 3072], P(None, 'dp', 'mp')
- up_bias_grad: float32 [2, 2, 1536], P(None, 'mp', 'dp')
- down_weight_grad: float32 [2, 3072, 768], P(None, 'mp', 'dp')
- out_bias_grad: float32 [2, 2, 768], P(None, None, ('dp', 'mp'))
- norm_gain_grad: float32 [2, 2, 768], P(None, None, ('dp', 'mp'))
- norm_shift_grad: float32 [2, 2, 768], P(None, None, ('dp', 'mp'))
The draws below stay inside these ranges and needn't reach their ends.
Inputs may be any that keep to these rules, and one draw needn't show every extreme that they name: `clip_lengths`: the 8 entries of one group sum to 512. A group holds either 8 clips, each strictly within 32 of 64 frames, or one clip of 512 frames followed by empty entries; one group in every eight is of the second kind. `live_lengths`: each entry is at most the clip's length and at least that length minus a quarter of it (rounded down); clips of 512 frames are not padded.
All inputs are finite; a program needn't handle non-finite values.
Results may differ from the reference program's by a relative error of at most 0.04.
Values may be sent and summed in bfloat16 or wider, within the bound.
No kernel may reach another device: no remote copies, remote signals or barrier semaphores. Data moves between devices by JAX's collectives and lax.ppermute only.
A program may use at most 192 MiB of HBM per device.

```python
import jax
import jax.numpy as jnp
from jax import lax

D = 768
H = 12
HD = 64
FF = 3072
LAYERS = 2
TOK_DEV = 512
CLIPS_DEV = 8
TOKENS = 8192
GROUPS = 2
D_GROUP = 384
FF_GROUP = 1536
N_DP = 16


def clip_table(key):
    long_pick = jax.random.randint(jax.random.fold_in(key, 101), (), 0, 8)
    base_length = TOK_DEV // CLIPS_DEV
    jitter = jax.random.randint(jax.random.fold_in(key, 102), (N_DP, CLIPS_DEV), 0, base_length // 2)
    short_lengths = base_length + jitter - jnp.roll(jitter, 1, axis=1)
    device = jnp.arange(N_DP, dtype=jnp.int32)
    single = jnp.where(jnp.arange(CLIPS_DEV, dtype=jnp.int32) == 0, TOK_DEV, 0)
    chosen = (device % 8 == long_pick)[:, None]
    return jnp.where(chosen, single[None, :], short_lengths).astype(jnp.int32)


def draw_clip_lengths(key, part):
    table = clip_table(key)
    return table.reshape(-1)


def draw_live_lengths(key, part):
    table = clip_table(key)
    key = jax.random.fold_in(key, 4)
    padding = jax.random.randint(key, table.shape, 0, table // 4 + 1)
    padding = jnp.where(table == TOK_DEV, 0, padding)
    return (table - padding).reshape(-1).astype(jnp.int32)


def raised(result, rng, source, target, blocks, factor):
    owner, partner = [(jnp.arange(result.shape[dim]) // (result.shape[dim] // blocks)).reshape([-1 if axis == dim else 1 for axis in range(result.ndim)]) for dim in (source, target)]
    chosen = jax.random.permutation(rng, blocks)[partner]
    strong = (owner == chosen) | (owner == (partner + blocks // 2) % blocks)
    return jnp.where(strong, factor * result, result)


def block_scale(stream_key, extent, shards, low, largest):
    level = 1.0
    for dim, parts in shards:
        heights = jax.random.uniform(jax.random.fold_in(jax.random.fold_in(stream_key, 6), dim), (parts,), jnp.float32, low / len(shards), largest / len(shards))
        level = level * jnp.repeat(jnp.exp(heights), extent[dim] // parts).reshape((-1,) + (1,) * (len(extent) - 1 - dim))
    return level


def bell_draw(own_key, shape, deviation, bound, cuts=(), held_as=jnp.bfloat16):
    drawn = jax.random.normal(own_key, shape, jnp.float32) * deviation
    if len(cuts) > 0:
        drawn = block_scale(own_key, shape, cuts, -0.22, 0.18) * drawn
    return jnp.clip(drawn, min=-bound, max=bound).astype(held_as)


def heavy_noise(rng, shape, width, bound, split, heavy, kind=jnp.bfloat16):
    values = width * jax.random.normal(rng, shape, jnp.float32)
    if split:
        values = values * block_scale(rng, shape, split, -0.22, 0.18)
    return jnp.clip(raised(values, jax.random.fold_in(rng, 3), *heavy), -bound, bound).astype(kind)


def setup_inputs(seed: int = 0) -> dict:
    keys = jax.random.split(jax.random.key(seed), 14)
    frames = bell_draw(keys[0], (TOKENS, D), 1.0, 6.0, ((0, 32),))
    qkv_weight = bell_draw(keys[1], (LAYERS, D, 3, D), D ** -0.5, 0.21875, ((3, 2),))
    qv_bias = bell_draw(keys[2], (LAYERS, 2, D), 0.3, 1.75, ((2, 2),), jnp.float32)
    out_weight = bell_draw(keys[3], (LAYERS, D, D), (D // 16) ** -0.5, 0.875, ((1, 2),))
    up_weight = bell_draw(keys[4], (LAYERS, D, FF), D ** -0.5, 0.21875, ((2, 2),))
    up_bias = bell_draw(keys[5], (LAYERS, FF), 0.5, 3.0, ((1, 2),), jnp.float32)
    down_weight = bell_draw(keys[6], (LAYERS, FF, D), (FF // 2) ** -0.5, 0.15625, ((1, 2),))
    out_bias = bell_draw(keys[7], (LAYERS, 2, D), 0.3, 1.75, (), jnp.float32)
    norm_gain = jnp.clip(1.0 + 0.15 * jax.random.normal(keys[8], (LAYERS, 2, D), jnp.float32), 0.25, 1.75)
    norm_shift = bell_draw(keys[9], (LAYERS, 2, D), 0.3, 1.75, (), jnp.float32)
    clip_lengths = draw_clip_lengths(jax.random.fold_in(keys[13], 71), 0)
    live_lengths = draw_live_lengths(jax.random.fold_in(keys[13], 71), 0)
    out_grad = heavy_noise(keys[12], (TOKENS, D), 1.0, 12.0, ((0, 32),), (0, 1, 32, 2.75))
    return dict(frames=frames, qkv_weight=qkv_weight, qv_bias=qv_bias, out_weight=out_weight, up_weight=up_weight, up_bias=up_bias, down_weight=down_weight, out_bias=out_bias, norm_gain=norm_gain, norm_shift=norm_shift, clip_lengths=clip_lengths, live_lengths=live_lengths, out_grad=out_grad)


@jax.custom_vjp
def low(v):
    return lax.optimization_barrier(v.astype(jnp.bfloat16)).astype(jnp.float32)

@jax.custom_vjp
def low_back(v):
    return v

def low_keep(v):
    return (low(v), None)

def low_pass(kept, grad):
    return (grad,)

def back_keep(v):
    return (v, None)

def back_low(kept, grad):
    return (low(grad),)
low.defvjp(low_keep, low_pass)
low_back.defvjp(back_keep, back_low)
norm_eps = 1e-05
score_scale = 0.125
masked_score = -1e+30

def product(multiplier, multiplicand):
    return jnp.dot(multiplier, multiplicand, precision=lax.Precision.HIGHEST, preferred_element_type=jnp.float32)

def layer_norm(values, gain_row, shift_row):
    centred = values - lax.optimization_barrier(jnp.mean(values, axis=-1, keepdims=True))
    variance = lax.optimization_barrier(jnp.mean(centred * centred, axis=-1, keepdims=True))
    return centred * lax.rsqrt(variance + norm_eps) * gain_row + shift_row

def clip_mask(lengths, live_counts, frame_count):
    lengths = lengths.astype(jnp.int32)
    clip_ends = jnp.cumsum(lengths).astype(jnp.int32)
    clip_starts = clip_ends - lengths
    position = jnp.arange(frame_count, dtype=jnp.int32)
    segment = lax.optimization_barrier(jnp.sum((position[:, None] >= clip_ends[None, :]).astype(jnp.int32), axis=1))
    inside = (position[:, None] >= clip_starts[None, :]) & (position[:, None] < clip_ends[None, :])
    offset = position[:, None] - clip_starts[None, :]
    alive_frames = jnp.any(inside & (offset < live_counts.astype(jnp.int32)[None, :]), axis=1)
    return (segment[:, None] == segment[None, :]) & alive_frames[None, :]

def one_layer(inputs, allowed, weights):
    qkv_weight, qv_bias, out_weight, up_weight, up_bias, down_weight, out_bias, norm_gain, norm_shift = weights
    frame_count = inputs.shape[0]
    joint_bias = jnp.concatenate([qv_bias[0], jnp.zeros_like(qv_bias[0]), qv_bias[1]])
    projected = low(low_back(product(low(inputs), qkv_weight.reshape(D, 3 * D)) + joint_bias))
    projected = projected.reshape(frame_count, 3, H, HD)
    queries = projected[:, 0]
    keys_all = projected[:, 1]
    values_all = projected[:, 2]
    scores = low_back(jnp.einsum('qhd,khd->hqk', queries, keys_all, precision=lax.Precision.HIGHEST) * score_scale)
    scores = jnp.where(allowed[None], scores, masked_score)
    highest = lax.optimization_barrier(jnp.max(scores, axis=-1, keepdims=True))
    weights_exp = jnp.exp(scores - highest)
    probabilities = weights_exp / lax.optimization_barrier(jnp.sum(weights_exp, axis=-1, keepdims=True))
    mixture = jnp.einsum('hqk,khd->qhd', low(probabilities), values_all, precision=lax.Precision.HIGHEST)
    mixture = low(low_back(mixture.reshape(frame_count, D)))
    hidden = inputs + low_back(product(mixture, out_weight)) + out_bias[0]
    first = layer_norm(hidden, norm_gain[0], norm_shift[0])
    up_value = low_back(product(low(first), up_weight) + up_bias)
    activated = jax.nn.gelu(up_value, approximate=False)
    second = first + low_back(product(low(activated), down_weight)) + out_bias[1]
    return layer_norm(second, norm_gain[1], norm_shift[1])

def reference(frames, qkv_weight, qv_bias, out_weight, up_weight, up_bias, down_weight, out_bias, norm_gain, norm_shift, clip_lengths, live_lengths, out_grad):
    params = tuple((element.astype(jnp.float32) for element in (qkv_weight, qv_bias, out_weight, up_weight, up_bias, down_weight, out_bias, norm_gain, norm_shift)))
    inputs_all = frames.astype(jnp.float32).reshape(N_DP, TOK_DEV, D)
    cotangent = out_grad.astype(jnp.float32).reshape(N_DP, TOK_DEV, D)
    lengths_all = clip_lengths.astype(jnp.int32).reshape(N_DP, CLIPS_DEV)
    live_all = live_lengths.astype(jnp.int32).reshape(N_DP, CLIPS_DEV)

    def group_layers(weights, group_inputs, group_lengths, group_live):
        allowed = clip_mask(group_lengths, group_live, TOK_DEV)
        values = group_inputs
        for layer_index in range(LAYERS):
            values = one_layer(values, allowed, tuple((element[layer_index] for element in weights)))
        return values
    checked = jax.checkpoint(group_layers)

    def forward(weights, all_inputs):

        def scan_step(carried, element):
            return (carried, checked(weights, element[0], element[1], element[2]))
        unused, outputs = lax.scan(scan_step, jnp.zeros((), jnp.float32), (all_inputs, lengths_all, live_all))
        return outputs
    outputs, pullback = jax.vjp(forward, params, inputs_all)
    weight_grads, input_grad = pullback(cotangent)
    qkv_grad, qv_grad, out_grad_w, up_grad, up_bias_g, down_grad, out_bias_g, gain_grad, shift_grad = weight_grads
    qv_bias_grad = qv_grad.reshape(LAYERS, 2, GROUPS, D_GROUP).transpose(0, 2, 1, 3)
    up_bias_grad = up_bias_g.reshape(LAYERS, GROUPS, FF_GROUP)
    return (outputs.reshape(TOKENS, D).astype(jnp.bfloat16), input_grad.reshape(TOKENS, D), qkv_grad, qv_bias_grad, out_grad_w, up_grad, up_bias_grad, down_grad, out_bias_g, gain_grad, shift_grad)
```

```python
import jax
import jax.numpy as jnp
from jax import lax
from jax.sharding import PartitionSpec as P

HD = 64


norm_eps = 1e-05
score_scale = 0.125
masked_score = -1e30
root_half = 0.7071067811865476
density_scale = 0.3989422804014327


def clip_mask(lengths, live_counts, frame_count):
    clip_ends = jnp.cumsum(lengths)
    clip_starts = clip_ends - lengths
    position = jnp.arange(frame_count, dtype=jnp.int32)
    segment = jnp.sum((position[:, None] >= clip_ends[None, :]).astype(jnp.int32), axis=1)
    inside = (position[:, None] >= clip_starts[None, :]) & (position[:, None] < clip_ends[None, :])
    offset = position[:, None] - clip_starts[None, :]
    alive_frames = jnp.any(inside & (offset < live_counts[None, :]), axis=1)
    return (segment[:, None] == segment[None, :]) & alive_frames[None, :]


def norm_forward(values, gain_row, shift_row):
    centred = values - jnp.mean(values, axis=-1, keepdims=True)
    inverse = lax.rsqrt(jnp.mean(centred * centred, axis=-1, keepdims=True) + norm_eps)
    normed = centred * inverse
    return (normed * gain_row + shift_row, normed, inverse)


def norm_backward(gradient, normed, inverse, gain_row):
    scaled = gradient * gain_row
    centred = (
        scaled
        - jnp.mean(scaled, axis=-1, keepdims=True)
        - normed * jnp.mean(scaled * normed, axis=-1, keepdims=True)
    )
    return (centred * inverse, jnp.sum(gradient * normed, axis=0), jnp.sum(gradient, axis=0))


def gelu_slope(values):
    normal_cdf = 0.5 * (1.0 + lax.erf(values * root_half))
    return normal_cdf + values * jnp.exp(-0.5 * values * values) * density_scale


def split_heads(projected):
    frame_count = projected.shape[0]
    head_count = projected.shape[2] // HD
    return tuple(
        (projected[:, part_index].reshape(frame_count, head_count, HD) for part_index in range(3))
    )


def block_scores(queries, keys_all, allowed):
    scores = (
        jnp.einsum("qhd,khd->hqk", queries, keys_all, preferred_element_type=jnp.float32)
        * score_scale
    )
    return (queries, jnp.where(allowed[None], scores, masked_score))


def attend(projected, allowed, block_rows):
    queries, keys_all, values_all = split_heads(projected)
    frame_count = queries.shape[0]

    def one_block(offset):
        rows_now, scores = block_scores(queries, keys_all, allowed)
        highest = jnp.max(scores, axis=-1, keepdims=True)
        weights_exp = jnp.exp(scores - highest)
        weight_total = jnp.sum(weights_exp, axis=-1, keepdims=True)
        probabilities = (weights_exp / weight_total).astype(jnp.bfloat16)
        mixture = jnp.einsum(
            "hqk,khd->qhd", probabilities, values_all, preferred_element_type=jnp.float32
        )
        return (
            mixture.reshape(block_rows, -1).astype(jnp.bfloat16),
            (highest + jnp.log(weight_total))[..., 0],
        )

    offsets = jnp.arange(frame_count // block_rows, dtype=jnp.int32) * block_rows
    mixture, log_totals = lax.map(one_block, offsets)
    return (mixture.reshape(frame_count, -1), log_totals)


def attend_back(projected, allowed, log_totals, grad_mixture, block_rows):
    queries, keys_all, values_all = split_heads(projected)
    frame_count = queries.shape[0]
    head_count = queries.shape[1]
    grad_heads = grad_mixture.reshape(frame_count, head_count, HD)

    def one_block(carried, element):
        grad_keys, grad_values = carried
        offset, block_totals = element
        rows_now, scores = block_scores(queries, keys_all, allowed)
        probabilities = jnp.exp(scores - block_totals[..., None])
        grad_probs = jnp.einsum(
            "qhd,khd->hqk", grad_heads, values_all, preferred_element_type=jnp.float32
        )
        grad_scores = (
            probabilities
            * (grad_probs - jnp.sum(probabilities * grad_probs, axis=-1, keepdims=True))
        ).astype(jnp.bfloat16)
        grad_values = grad_values + jnp.einsum(
            "hqk,qhd->khd",
            probabilities.astype(jnp.bfloat16),
            grad_heads,
            preferred_element_type=jnp.float32,
        )
        grad_keys = (
            grad_keys
            + jnp.einsum("hqk,qhd->khd", grad_scores, rows_now, preferred_element_type=jnp.float32)
            * score_scale
        )
        grad_rows = (
            jnp.einsum("hqk,khd->qhd", grad_scores, keys_all, preferred_element_type=jnp.float32)
            * score_scale
        )
        return ((grad_keys, grad_values), grad_rows)

    empty = jnp.zeros((frame_count, head_count, HD), jnp.float32)
    offsets = jnp.arange(frame_count // block_rows, dtype=jnp.int32) * block_rows
    (grad_keys, grad_values), grad_rows = lax.scan(one_block, (empty, empty), (offsets, log_totals))
    stacked = jnp.stack(
        [
            grad_rows.reshape(frame_count, -1),
            grad_keys.reshape(frame_count, -1),
            grad_values.reshape(frame_count, -1),
        ],
        axis=1,
    )
    return stacked.astype(jnp.bfloat16)


def swap(part):
    return lax.ppermute(part, "mp", [(0, 1), (1, 0)])


def pair_sum(part):
    low_part = part.astype(jnp.bfloat16)
    return low_part.astype(jnp.float32) + swap(low_part).astype(jnp.float32)


def stream_order(bits, first_bits):
    order = list(first_bits) + [b for b in range(bits) if b not in first_bits]
    places = []
    for place in range(1 << bits):
        block = 0
        for position, bit in enumerate(order):
            if (place >> (bits - 1 - position)) & 1:
                block |= 1 << bit
        places.append(block)
    return order, places


def ordered_rows(factor, places):
    shards = len(places)
    turned = factor.T.reshape(shards, factor.shape[1] // shards, factor.shape[0])
    index = jnp.asarray(places, jnp.int32) ^ lax.axis_index("dp")
    return turned[index].reshape(factor.shape[1], factor.shape[0])


def sum_rows(total, order):
    count = lax.axis_size("dp")
    for step, bit in enumerate(order):
        half = total.shape[0] // 2
        got = lax.ppermute(total[half:], "dp", [(i, i ^ (1 << bit)) for i in range(count)])
        total = total[:half].astype(jnp.float32) + got.astype(jnp.float32)
        if step < len(order) - 1:
            total = total.astype(jnp.bfloat16)
    return total


def matrix_grad(factor, others, first_bits):
    count = lax.axis_size("dp")
    bits = count.bit_length() - 1
    order, places = stream_order(bits, [b for b in first_bits if b < bits])
    rows = ordered_rows(factor[0], places)
    grads = [jnp.dot(rows, others[0], preferred_element_type=jnp.float32).astype(jnp.bfloat16)]
    for more, other in zip(factor[1:], others[1:]):
        grads.append(
            jnp.dot(ordered_rows(more, places), other, preferred_element_type=jnp.float32).astype(jnp.bfloat16)
        )
    joint = grads[0] if len(grads) == 1 else jnp.concatenate(grads, axis=1)
    return sum_rows(joint, order)


def on_device(
    frames,
    qkv_weight,
    qv_bias,
    out_weight,
    up_weight,
    up_bias,
    down_weight,
    out_bias,
    norm_gain,
    norm_shift,
    clip_lengths,
    live_lengths,
    out_grad,
):
    layer_count = qkv_weight.shape[0]
    model_width = qkv_weight.shape[1]
    group_width = qkv_weight.shape[3]
    row_count = frames.shape[0]
    frame_count = row_count * lax.axis_size("mp")
    shards = lax.axis_size("dp")
    block_rows = min(512, frame_count)
    allowed = clip_mask(clip_lengths, live_lengths, frame_count)
    inputs_all = lax.all_gather(frames, "mp", axis=0, tiled=True)
    grad_all = lax.all_gather(out_grad, "mp", axis=0, tiled=True)
    residual = inputs_all.astype(jnp.float32)
    own_start = lax.axis_index("mp") * row_count
    saved = []
    for layer_index in range(layer_count):
        joint_weight = qkv_weight[layer_index].reshape(model_width, 3 * group_width)
        joint_bias = jnp.concatenate(
            [
                qv_bias[layer_index, 0],
                jnp.zeros_like(qv_bias[layer_index, 0]),
                qv_bias[layer_index, 1],
            ]
        )
        projected = (
            jnp.dot(inputs_all, joint_weight, preferred_element_type=jnp.float32) + joint_bias
        ).astype(jnp.bfloat16)
        projected = projected.reshape(frame_count, 3, group_width)
        mixture_low, log_totals = attend(projected, allowed, block_rows)
        attn = pair_sum(jnp.dot(mixture_low, out_weight[layer_index], preferred_element_type=jnp.float32))
        hidden = residual + attn + out_bias[layer_index, 0]
        first, normed_first, inverse_first = norm_forward(
            hidden, norm_gain[layer_index, 0], norm_shift[layer_index, 0]
        )
        first_all = first.astype(jnp.bfloat16)
        up_value = (
            jnp.dot(first_all, up_weight[layer_index], preferred_element_type=jnp.float32)
            + up_bias[layer_index]
        )
        activated = jax.nn.gelu(up_value, approximate=False).astype(jnp.bfloat16)
        ffn = pair_sum(jnp.dot(activated, down_weight[layer_index], preferred_element_type=jnp.float32))
        second = first + ffn + out_bias[layer_index, 1]
        output_rows, normed_second, inverse_second = norm_forward(
            second, norm_gain[layer_index, 1], norm_shift[layer_index, 1]
        )
        saved.append(
            (
                inputs_all,
                projected,
                log_totals,
                mixture_low,
                normed_first,
                inverse_first,
                first_all,
                up_value,
                activated,
                normed_second,
                inverse_second,
            )
        )
        residual = output_rows
        inputs_all = output_rows.astype(jnp.bfloat16)
    frames_out = lax.dynamic_slice_in_dim(inputs_all, own_start, row_count, 0)
    gradient = grad_all.astype(jnp.float32)
    layer_terms = [None] * layer_count
    vector_terms = []
    wide_terms = []
    for layer_index in reversed(range(layer_count)):
        (
            inputs_all,
            projected,
            log_totals,
            mixture_low,
            normed_first,
            inverse_first,
            first_all,
            up_value,
            activated,
            normed_second,
            inverse_second,
        ) = saved[layer_index]
        dsecond, gain_second, shift_second = norm_backward(
            gradient, normed_second, inverse_second, norm_gain[layer_index, 1]
        )
        bias_second = jnp.sum(dsecond, axis=0)
        dffn_all = dsecond.astype(jnp.bfloat16)
        dactivated = jnp.einsum(
            "td,fd->tf", dffn_all, down_weight[layer_index], preferred_element_type=jnp.float32
        )
        dup_low = (dactivated * gelu_slope(up_value)).astype(jnp.bfloat16)
        up_bias_grad = jnp.sum(dup_low, axis=0, dtype=jnp.float32)
        dfirst = dsecond + pair_sum(
            jnp.einsum("tf,df->td", dup_low, up_weight[layer_index], preferred_element_type=jnp.float32)
        )
        down_out = matrix_grad([dffn_all], [activated], [0, 1, 2, 3])
        up_out = matrix_grad([first_all], [dup_low], [1, 2, 0, 3])
        dhidden, gain_first, shift_first = norm_backward(
            dfirst, normed_first, inverse_first, norm_gain[layer_index, 0]
        )
        bias_first = jnp.sum(dhidden, axis=0)
        dattn_all = dhidden.astype(jnp.bfloat16)
        dmixture = jnp.einsum(
            "td,gd->tg", dattn_all, out_weight[layer_index], preferred_element_type=jnp.float32
        ).astype(jnp.bfloat16)
        dprojected = attend_back(projected, allowed, log_totals, dmixture, block_rows)
        q_sum = jnp.sum(dprojected[:, 0], axis=0, dtype=jnp.float32)
        v_sum = jnp.sum(dprojected[:, 2], axis=0, dtype=jnp.float32)
        flat_grad = dprojected.reshape(frame_count, 3 * group_width)
        joint_weight = qkv_weight[layer_index].reshape(model_width, 3 * group_width)
        gradient = dhidden + pair_sum(
            jnp.einsum("te,de->td", flat_grad, joint_weight, preferred_element_type=jnp.float32)
        )
        attn_out = matrix_grad([dattn_all, inputs_all], [mixture_low, flat_grad], [2, 0, 1, 3])
        layer_terms[layer_index] = (down_out, up_out, attn_out)
        vector_terms = [bias_first, bias_second, gain_first, gain_second, shift_first, shift_second] + vector_terms
        wide_terms = [q_sum, v_sum, up_bias_grad] + wide_terms
    input_grad = lax.dynamic_slice_in_dim(gradient, own_start, row_count, 0)
    wide = jnp.concatenate(
        [w.reshape(shards, w.shape[0] // shards) for w in wide_terms], axis=1
    )
    narrow = jnp.stack(vector_terms).reshape(len(vector_terms), shards, -1)
    narrow = jnp.transpose(narrow, (1, 0, 2)).reshape(shards, -1)
    small = jnp.concatenate([narrow, wide], axis=1).astype(jnp.bfloat16)
    small = lax.all_to_all(small, "dp", 0, 0, tiled=True)
    small = jnp.sum(small.astype(jnp.float32), axis=0)
    split = narrow.shape[1]
    piece = model_width // shards
    vectors = small[:split].reshape(layer_count, 3, 2, piece)
    own = piece // lax.axis_size("mp")
    vectors = lax.dynamic_slice_in_dim(vectors, lax.axis_index("mp") * own, own, 3)
    wide_out = small[split:].reshape(layer_count, -1)
    q_piece = group_width // shards
    qv_out = wide_out[:, : 2 * q_piece].reshape(layer_count, 1, 2, q_piece)
    up_bias_out = wide_out[:, 2 * q_piece :].reshape(layer_count, 1, -1)
    down_out = jnp.stack([t[0].T for t in layer_terms])
    up_out = jnp.stack([t[1] for t in layer_terms])
    out_weight_out = jnp.stack([t[2][:, :group_width].T for t in layer_terms])
    qkv_out = jnp.stack([t[2][:, group_width:].reshape(piece, 3, group_width) for t in layer_terms])
    return (
        frames_out,
        input_grad,
        qkv_out,
        qv_out,
        out_weight_out,
        up_out,
        up_bias_out,
        down_out,
        vectors[:, 0],
        vectors[:, 1],
        vectors[:, 2],
    )


def solution(mesh):
    placed = (
        P(("dp", "mp"), None),
        P(None, None, None, "mp"),
        P(None, None, "mp"),
        P(None, "mp", None),
        P(None, None, "mp"),
        P(None, "mp"),
        P(None, "mp", None),
        P(),
        P(),
        P(),
        P("dp"),
        P("dp"),
        P(("dp", "mp"), None),
    )
    return jax.shard_map(
        on_device,
        mesh=mesh,
        in_specs=placed,
        out_specs=(
            P(("dp", "mp"), None),
            P(("dp", "mp"), None),
            P(None, "dp", None, "mp"),
            P(None, "mp", None, "dp"),
            P(None, "mp", "dp"),
            P(None, "dp", "mp"),
            P(None, "mp", "dp"),
            P(None, "mp", "dp"),
            P(None, None, ("dp", "mp")),
            P(None, None, ("dp", "mp")),
            P(None, None, ("dp", "mp")),
        ),
        check_vma=False,
    )
```

```python
import functools

import jax
import jax.numpy as jnp
from jax import lax
from jax.experimental import pallas as pl
from jax.experimental.pallas import tpu as pltpu
from jax.sharding import PartitionSpec as P

HD = 64
LANES = 128
MIB = 1 << 20


norm_eps = 1e-05
score_scale = 0.125
masked_score = -1e30
root_half = 0.7071067811865476
density_scale = 0.3989422804014327
f32 = jnp.float32
bf16 = jnp.bfloat16


def dot_nn(left, right):
    return lax.dot_general(left, right, (((1,), (0,)), ((), ())), preferred_element_type=f32)


def dot_nt(left, right):
    return lax.dot_general(left, right, (((1,), (1,)), ((), ())), preferred_element_type=f32)


def shaped(shape, dtype):
    return jax.ShapeDtypeStruct(shape, dtype)


def staged_call(kernel, name, inputs, outs, scratch, flops, megabytes=56):
    operands, specs, buffers, kinds = [], [], [], []
    copy_count = 0
    for entry in inputs:
        if len(entry) == 1:
            operands.append(entry[0])
            specs.append(pl.BlockSpec(memory_space=pltpu.SMEM))
            kinds.append(("scalar", len(operands) - 1))
        elif len(entry) == 2:
            operands.append(entry[0])
            specs.append(pl.BlockSpec(memory_space=pl.ANY))
            picked = 0 if entry[1] is None else len(entry[1]) if isinstance(entry[1], tuple) else 1
            shape = entry[0].shape[picked:]
            kinds.append(("whole", len(operands) - 1, entry[1], len(buffers), copy_count))
            buffers.append(pltpu.VMEM(shape, entry[0].dtype))
            copy_count += 1
        else:
            operands += list(entry)
            specs += [pl.BlockSpec(memory_space=pl.ANY)] * 2 + [pl.BlockSpec(memory_space=pltpu.SMEM)]
            rows, columns = entry[0].shape
            kinds.append(("halves", len(operands) - 3, rows, len(buffers), copy_count))
            buffers.append(pltpu.VMEM((2 * rows, columns), entry[0].dtype))
            copy_count += 2

    def body(*refs):
        in_refs, refs = refs[: len(operands)], refs[len(operands) :]
        out_refs, refs = refs[: len(outs)], refs[len(outs) :]
        in_buffers, refs = refs[: len(buffers)], refs[len(buffers) :]
        out_buffers, refs = refs[: len(outs)], refs[len(outs) :]
        in_sem, out_sem = refs[-2:]
        getters = []
        for kind in kinds:
            if kind[0] == "scalar":
                getters.append(in_refs[kind[1]])
                continue
            buffer = in_buffers[kind[3]]
            if kind[0] == "whole":
                source = in_refs[kind[1]]
                if kind[2] is not None:
                    source = source.at[kind[2]]
                copies = [pltpu.make_async_copy(source, buffer, in_sem.at[kind[4]])]
            else:
                rows = kind[2]
                core = in_refs[kind[1] + 2][0]
                copies = [
                    pltpu.make_async_copy(
                        in_refs[kind[1] + which],
                        buffer.at[pl.ds(pl.multiple_of((core ^ which) * rows, rows), rows)],
                        in_sem.at[kind[4] + which],
                    )
                    for which in range(2)
                ]
            for copy in copies:
                copy.start()
            getters.append(Arriving(buffer, copies))
        leaving = [Leaving(buffer, ref, out_sem.at[i]) for i, (buffer, ref) in enumerate(zip(out_buffers, out_refs))]
        kernel(getters, leaving, refs[:-2])
        for getter in getters:
            if isinstance(getter, Arriving):
                getter.get()
        for out in leaving:
            out.send()
        for out in leaving:
            out.finish()

    moved = sum(a.size * a.dtype.itemsize for a in [*operands, *outs])
    return pl.pallas_call(
        body,
        name=name,
        in_specs=specs,
        out_specs=[pl.BlockSpec(memory_space=pl.ANY)] * len(outs),
        out_shape=outs,
        scratch_shapes=buffers
        + [pltpu.VMEM(out.shape, out.dtype) for out in outs]
        + list(scratch)
        + [pltpu.SemaphoreType.DMA((max(copy_count, 1),)), pltpu.SemaphoreType.DMA((len(outs),))],
        compiler_params=pltpu.CompilerParams(vmem_limit_bytes=megabytes * MIB),
        cost_estimate=pl.CostEstimate(flops=int(flops), bytes_accessed=int(moved), transcendentals=0),
    )(*operands)


class Arriving:
    def __init__(self, buffer, copies):
        self.buffer, self.copies = buffer, copies

    def get(self):
        for copy in self.copies:
            copy.wait()
        self.copies = []
        return self.buffer


class Leaving:
    def __init__(self, buffer, target, sem):
        self.ref = buffer
        self.copy = pltpu.make_async_copy(buffer, target, sem)
        self.sent = False

    def send(self):
        if not self.sent:
            self.copy.start()
        self.sent = True

    def finish(self):
        self.copy.wait()


def normal_cdf(values):
    return 0.5 * (1.0 + lax.erf(values * root_half))


def norm_forward(values):
    centred = values - jnp.mean(values, axis=-1, keepdims=True)
    inverse = lax.rsqrt(jnp.mean(centred * centred, axis=-1, keepdims=True) + norm_eps)
    return centred * inverse, inverse


def norm_backward(gradient, normed, inverse, gain_row):
    scaled = gradient * gain_row
    centred = (
        scaled
        - jnp.mean(scaled, axis=-1, keepdims=True)
        - normed * jnp.mean(scaled * normed, axis=-1, keepdims=True)
    )
    return centred * inverse


def mask_features(clip_ref, live_ref, frame_count):
    clips = clip_ref.shape[0]
    lane = lax.broadcasted_iota(jnp.int32, (8, LANES), 1)
    key_low = jnp.zeros((8, LANES), jnp.int32)
    key_high = jnp.zeros((8, LANES), jnp.int32)
    own_low = jnp.zeros((8, LANES), jnp.int32)
    own_high = jnp.zeros((8, LANES), jnp.int32)
    start = jnp.int32(0)
    for clip in range(clips):
        end = start + clip_ref[clip]
        alive = start + live_ref[clip]
        here = lane == clip
        dead = lane == clip + clips
        key_low = jnp.where(here, start, jnp.where(dead, alive, key_low))
        key_high = jnp.where(here, alive, jnp.where(dead, end, key_high))
        own_low = jnp.where(here, start, own_low)
        own_high = jnp.where(here, end, own_high)
        start = end
    position = lax.broadcasted_iota(jnp.int32, (frame_count, LANES), 0)
    lane = lax.broadcasted_iota(jnp.int32, (frame_count, LANES), 1)
    key_in = (position >= key_low[:1]) & (position < key_high[:1])
    own = ((position >= own_low[:1]) & (position < own_high[:1])) | (lane >= 2 * clips)
    keys = jnp.where(key_in, 1.0, 0.0).astype(bf16)
    queries = jnp.where(own, 0.0, masked_score).astype(bf16)
    return keys, queries


def half_lanes(values, half):
    lane = lax.broadcasted_iota(jnp.int32, values.shape, 1)
    keep = (lane < HD) if half == 0 else (lane >= HD)
    return jnp.where(keep, values, jnp.zeros_like(values))


def add_norm(layer, which, before, own, got, rows_of, outs, rows=128):
    own_ref, got_ref = own.get(), got.get()
    bias_ref, gain_ref, shift_ref = (entry.get() for entry in rows_of)
    bias = bias_ref[layer, which][None]
    gain = gain_ref[layer, which][None]
    shift = shift_ref[layer, which][None]
    before_ref = before[0].get()
    normed_ref, inverse_ref, low_ref = (out.ref for out in outs)

    @pl.loop(0, own_ref.shape[0] // rows)
    def _(step):
        now = pl.ds(pl.multiple_of(step * rows, rows), rows)
        residual = before_ref[now, :].astype(f32)
        if len(before) > 1:
            residual = residual * gain_ref[before[1], before[2]][None] + shift_ref[before[1], before[2]][None]
        total = residual + (own_ref[now, :].astype(f32) + got_ref[now, :].astype(f32)) + bias
        normed, inverse = norm_forward(total)
        normed_ref[now, :] = normed
        inverse_ref[now, :] = jnp.broadcast_to(inverse, (rows, LANES))
        low_ref[now, :] = (normed * gain + shift).astype(bf16)

    for out in outs:
        out.send()


def attention_forward_kernel(layer, ins, outs, scratch):
    clips, lives, queries, keys, values, out_weight, qv_bias = ins[:7]
    qkv, lse, mix, part, low = outs[:5]
    mixt_ref, valt_ref = scratch
    qkv_ref, frames = qkv.ref, low.ref.shape[0]
    group = mix.ref.shape[1]
    if layer == 0:
        low.ref[...] = ins[7].get()[...]
        low.send()
    else:
        before, own, got = ins[7:10]
        add_norm(layer - 1, 1, (before, layer - 1, 0), own, got, ins[10:13], [outs[5], outs[6], low])
    key_features, query_features = mask_features(clips, lives, frames)
    rows = low.ref[...]
    for part_index, weight in enumerate((queries, keys, values)):
        columns = slice(part_index * group, (part_index + 1) * group)
        value = dot_nn(rows, weight.get()[...])
        if part_index != 1:
            value = value + qv_bias.get()[layer, part_index // 2][None]
        value = value.astype(bf16)
        if part_index == 0:
            value = value * jnp.asarray(score_scale, bf16)
        qkv_ref[:, columns] = value
        if part_index == 2:
            valt_ref[...] = value.T
    qkv.send()
    for pair in range(group // LANES):
        query_pair = qkv_ref[:, pair * LANES : (pair + 1) * LANES]
        key_pair = qkv_ref[:, group + pair * LANES : group + (pair + 1) * LANES]
        key_wide = jnp.concatenate([key_pair, key_features], axis=1)
        for half in range(2):
            head = 2 * pair + half
            query_wide = jnp.concatenate([half_lanes(query_pair, half), query_features], axis=1)
            scores = dot_nt(key_wide, query_wide)
            highest = jnp.max(scores, axis=0, keepdims=True)
            weights = jnp.exp(scores - highest)
            total = jnp.sum(weights, axis=0, keepdims=True)
            rows = slice(head * HD, (head + 1) * HD)
            mixed = dot_nn(valt_ref[rows, :], weights.astype(bf16))
            mixt_ref[rows, :] = mixed / total
            lse.ref[head : head + 1, :] = highest + jnp.log(total)
    lse.send()
    mixture = mixt_ref[...].T.astype(bf16)
    mix.ref[...] = mixture
    mix.send()
    part.ref[...] = dot_nn(mixture, out_weight.get()[...]).astype(bf16)


def attention_forward(layer, clips, lives, weights, rows):
    qkv_weight, out_weight, qv_bias, norm_rows = weights
    group = out_weight.shape[1]
    if layer == 0:
        frames, width = 2 * rows[0].shape[0], rows[0].shape[1]
        first = [tuple(rows)]
    else:
        frames, width = rows[0].shape
        first = [(array, None) for array in (*rows, *norm_rows)]
    inputs = [
        (clips,), (lives,), *[(qkv_weight, (layer, part)) for part in range(3)], (out_weight, layer),
        (qv_bias, None), *first,
    ]
    outs = [
        shaped((frames, 3 * group), bf16),
        shaped((8 * pl.cdiv(group // HD, 8), frames), f32),
        shaped((frames, group), bf16),
        shaped((frames, width), bf16),
        shaped((frames, width), bf16),
    ]
    if layer > 0:
        outs += [shaped((frames, width), f32), shaped((frames, LANES), f32)]
    scratch = [pltpu.VMEM((group, frames), f32), pltpu.VMEM((group, frames), bf16)]
    flops = 2 * frames * width * 4 * group + 4 * frames * frames * group * 2
    return staged_call(
        functools.partial(attention_forward_kernel, layer), "attention", inputs, outs, scratch, flops
    )


def ffn_forward_kernel(layer, ins, outs, scratch):
    before, own, got = ins[:3]
    up_weight, down_weight, up_bias = ins[6:9]
    normed, inverse, low, up, act, part = outs
    source = (before,) if layer == 0 else (before, layer - 1, 1)
    add_norm(layer, 0, source, own, got, ins[3:6], [normed, inverse, low])
    rows = low.ref[...]
    hidden = up.ref.shape[1]
    chunk = 512
    total = None
    for start in range(0, hidden, chunk):
        columns = slice(start, start + chunk)
        up_value = dot_nn(rows, up_weight.get()[:, columns]) + up_bias.get()[layer, columns][None]
        up.ref[:, columns] = up_value.astype(bf16)
        active = (up_value * normal_cdf(up_value)).astype(bf16)
        act.ref[:, columns] = active
        product = dot_nn(active, down_weight.get()[columns, :])
        total = product if total is None else total + product
    up.send()
    act.send()
    part.ref[...] = total.astype(bf16)


def ffn_forward(layer, weights, rows):
    up_weight, down_weight, up_bias, norm_rows = weights
    frames, width = rows[0].shape
    hidden = up_weight.shape[2]
    inputs = [
        *[(array, None) for array in (*rows, *norm_rows)], (up_weight, layer), (down_weight, layer), (up_bias, None)
    ]
    outs = [
        shaped((frames, width), f32),
        shaped((frames, LANES), f32),
        shaped((frames, width), bf16),
        shaped((frames, hidden), bf16),
        shaped((frames, hidden), bf16),
        shaped((frames, width), bf16),
    ]
    return staged_call(
        functools.partial(ffn_forward_kernel, layer), "ffn", inputs, outs, [], 4 * frames * width * hidden
    )


def norm_sums(sums, dy, normed, result):
    return tuple(
        total + jnp.sum(term, axis=0, keepdims=True) for total, term in zip(sums, (result, dy * normed, dy))
    )


def ffn_backward_kernel(layer, last, rows, ins, outs, scratch):
    dsecond, dlow, dup_out, part, vectors, wide = outs[:6]
    if last:
        core, grad, before, own, got, bias, gain, shift = ins[:8]
        before_ref, bias_ref, shift_ref = before.get(), bias.get(), shift.get()
    else:
        normed_in, inverse_in, grad, own, got, gain = ins[:6]
        normed_ref, inverse_ref = normed_in.get(), inverse_in.get()
    down_weight, up_weight, up_in = ins[-3:]
    grad_ref, own_ref, got_ref, gain_ref = grad.get(), own.get(), got.get(), gain.get()
    frames, width = own_ref.shape

    def norm_step(step, sums):
        now = pl.ds(pl.multiple_of(step * rows, rows), rows)
        both = own_ref[now, :].astype(f32) + got_ref[now, :].astype(f32)
        if last:
            residual = before_ref[now, :] * gain_ref[layer, 0][None] + shift_ref[layer, 0][None]
            normed, inverse = norm_forward(residual + both + bias_ref[layer, 1][None])
            scratch[0][now, :] = (normed * gain_ref[layer, 1][None] + shift_ref[layer, 1][None]).astype(bf16)
            dy = grad_ref[now, :].astype(f32)
        else:
            normed = normed_ref[now, :]
            inverse = inverse_ref[now, :][:, :1]
            dy = grad_ref[now, :] + both
        result = norm_backward(dy, normed, inverse, gain_ref[layer, 1][None])
        dsecond.ref[now, :] = result
        dlow.ref[now, :] = result.astype(bf16)
        return norm_sums(sums, dy, normed, result)

    zero = jnp.zeros((1, width), f32)
    sums = lax.fori_loop(0, frames // rows, norm_step, (zero, zero, zero))
    for row, value in enumerate(sums):
        vectors.ref[row : row + 1, :] = value
    dsecond.send()
    dlow.send()
    vectors.send()
    if last:
        half = frames // 2
        outs[6].ref[...] = scratch[0][pl.ds(pl.multiple_of(core[0] * half, half), half), :]
        outs[6].send()
    hidden = dup_out.ref.shape[1]
    low = dlow.ref[...]
    chunk = 512
    total = None
    for start in range(0, hidden, chunk):
        columns = slice(start, start + chunk)
        dactive = dot_nt(low, down_weight.get()[columns, :])
        up_value = up_in.get()[:, columns].astype(f32)
        slope = normal_cdf(up_value) + up_value * (jnp.exp(-0.5 * up_value * up_value) * density_scale)
        dup = (dactive * slope).astype(bf16)
        dup_out.ref[:, columns] = dup
        wide.ref[0:1, columns] = jnp.sum(dup.astype(f32), axis=0, keepdims=True)
        product = dot_nt(dup, up_weight.get()[:, columns])
        total = product if total is None else total + product
    dup_out.send()
    wide.send()
    part.ref[...] = total.astype(bf16)


def ffn_backward(layer, last, weights, rows, up_value, core):
    up_weight, down_weight, norm_rows = weights
    frames, width = rows[-1].shape
    hidden = up_weight.shape[2]
    if last:
        inputs = [(core,), (rows[0], rows[1], core)] + [(array, None) for array in (*rows[2:], *norm_rows)]
    else:
        inputs = [(array, None) for array in (*rows, norm_rows[1])]
    inputs += [(down_weight, layer), (up_weight, layer), (up_value, None)]
    outs = [
        shaped((frames, width), f32),
        shaped((frames, width), bf16),
        shaped((frames, hidden), bf16),
        shaped((frames, width), bf16),
        shaped((8, width), f32),
        shaped((8, hidden), f32),
    ]
    scratch = []
    if last:
        outs.append(shaped((frames // 2, width), bf16))
        scratch = [pltpu.VMEM((frames, width), bf16)]
    return staged_call(
        functools.partial(ffn_backward_kernel, layer, last, 128), "ffn_back", inputs, outs, scratch,
        4 * frames * width * hidden,
    )


def attention_backward_kernel(layer, rows, ins, outs, scratch):
    clips, lives, dsecond, own, got, normed_in, inverse_in, gain, out_weight, qkv, mix, lse = ins[:12]
    qkv_weights = ins[12:15]
    dhidden, dlow, dqkv, part, vectors, wide = outs
    dmix_ref, keyt_ref, dqt_ref, delta_ref = scratch
    dsecond_ref, own_ref, got_ref, normed_ref, inverse_ref, gain_ref = (
        entry.get() for entry in (dsecond, own, got, normed_in, inverse_in, gain)
    )
    frames, width = own_ref.shape
    group = dmix_ref.shape[1]

    def norm_step(step, sums):
        now = pl.ds(pl.multiple_of(step * rows, rows), rows)
        dy = dsecond_ref[now, :] + (own_ref[now, :].astype(f32) + got_ref[now, :].astype(f32))
        normed = normed_ref[now, :]
        result = norm_backward(dy, normed, inverse_ref[now, :][:, :1], gain_ref[layer, 0][None])
        dhidden.ref[now, :] = result
        dlow.ref[now, :] = result.astype(bf16)
        return norm_sums(sums, dy, normed, result)

    zero = jnp.zeros((1, width), f32)
    sums = lax.fori_loop(0, frames // rows, norm_step, (zero, zero, zero))
    for row, value in enumerate(sums):
        vectors.ref[row : row + 1, :] = value
    dhidden.send()
    dlow.send()
    vectors.send()
    key_features, query_features = mask_features(clips, lives, frames)
    dmix = dot_nt(dlow.ref[...], out_weight.get()[...]).astype(bf16)
    dmix_ref[...] = dmix
    qkv_ref, lse_ref = qkv.get(), lse.get()
    keyt_ref[...] = qkv_ref[:, group : 2 * group].T * jnp.asarray(score_scale, bf16)
    product = dmix.astype(f32) * mix.get()[...].astype(f32)
    high = product.astype(bf16)
    rest = (product - high.astype(f32)).astype(bf16)
    head_of = lax.broadcasted_iota(jnp.int32, (lse_ref.shape[0], group), 1) // HD
    row = lax.broadcasted_iota(jnp.int32, (lse_ref.shape[0], group), 0)
    pick = jnp.where(head_of == row, 1.0, 0.0).astype(bf16)
    delta_ref[...] = dot_nt(pick, high) + dot_nt(pick, rest)
    for pair in range(group // LANES):
        columns = [slice(part * group + pair * LANES, part * group + (pair + 1) * LANES) for part in range(3)]
        query_pair = qkv_ref[:, columns[0]]
        key_wide = jnp.concatenate([qkv_ref[:, columns[1]], key_features], axis=1)
        value_pair = qkv_ref[:, columns[2]]
        dmix_pair = dmix_ref[:, columns[0]]
        dkeys = dvalues = None
        for half in range(2):
            head = 2 * pair + half
            query_half = half_lanes(query_pair, half)
            dmix_half = half_lanes(dmix_pair, half)
            scores = dot_nt(key_wide, jnp.concatenate([query_half, query_features], axis=1))
            probs = jnp.exp(scores - lse_ref[head : head + 1, :])
            dprobs = dot_nt(value_pair, dmix_half)
            dscores = (probs * (dprobs - delta_ref[head : head + 1, :])).astype(bf16)
            dvalue = dot_nn(probs.astype(bf16), dmix_half)
            dkey = dot_nn(dscores, query_half)
            dvalues = dvalue if dvalues is None else dvalues + dvalue
            dkeys = dkey if dkeys is None else dkeys + dkey
            head_rows = slice(head * HD, (head + 1) * HD)
            dqt_ref[head_rows, :] = dot_nn(keyt_ref[head_rows, :], dscores)
        dqkv.ref[:, columns[1]] = dkeys.astype(bf16)
        dqkv.ref[:, columns[2]] = dvalues.astype(bf16)
    dqkv.ref[:, :group] = dqt_ref[...].T.astype(bf16)
    dqkv.send()
    total = None
    for part_index, weight in enumerate(qkv_weights):
        values = dqkv.ref[:, part_index * group : (part_index + 1) * group]
        if part_index != 1:
            wide.ref[part_index // 2 : part_index // 2 + 1, :] = jnp.sum(values.astype(f32), axis=0, keepdims=True)
        product = dot_nt(values, weight.get()[...])
        total = product if total is None else total + product
    part.ref[...] = total.astype(bf16)


def attention_backward(layer, clips, lives, weights, rows, saved):
    qkv_weight, out_weight, gain = weights
    frames, width = rows[0].shape
    group = out_weight.shape[1]
    inputs = [
        (clips,), (lives,), *[(array, None) for array in (*rows, gain)], (out_weight, layer),
        *[(array, None) for array in saved], *[(qkv_weight, (layer, part)) for part in range(3)],
    ]
    outs = [
        shaped((frames, width), f32),
        shaped((frames, width), bf16),
        shaped((frames, 3 * group), bf16),
        shaped((frames, width), bf16),
        shaped((8, width), f32),
        shaped((8, group), f32),
    ]
    scratch = [
        pltpu.VMEM((frames, group), bf16),
        pltpu.VMEM((group, frames), bf16),
        pltpu.VMEM((group, frames), f32),
        pltpu.VMEM(saved[2].shape, f32),
    ]
    flops = 2 * frames * width * 4 * group + 10 * frames * frames * group
    return staged_call(
        functools.partial(attention_backward_kernel, layer, 128), "attention_back", inputs, outs, scratch, flops
    )


def turned_rows(factor_ref, place_ref, stream, turned_ref):
    shards = place_ref.shape[1]
    piece = turned_ref.shape[0] // shards
    turned = factor_ref[...].T
    for shard in range(shards):
        start = pl.multiple_of(place_ref[stream, shard] * piece, piece)
        turned_ref[pl.ds(start, piece), :] = turned[shard * piece : (shard + 1) * piece, :]


def matrix_grad_kernel(streams, factor_count, ins, outs, scratch):
    place_ref = ins[0]
    factors, others = ins[1 : 1 + factor_count], ins[1 + factor_count :]
    scratch, outs = list(scratch), list(outs)
    for order, pieces in streams:
        if order is None:
            targets = [(outs.pop(0), slice(None))]
        else:
            half = scratch[0].shape[0] // 2
            targets = [(outs.pop(0), slice(half, 2 * half)), (outs.pop(0), slice(0, half))]
        first = 0
        for factor, other, start, end in pieces:
            turned_ref = scratch.pop(0)
            if order is None:
                turned_ref[...] = factors[factor].get()[...].T
            else:
                turned_rows(factors[factor].get(), place_ref, order, turned_ref)
            for out, rows in targets:
                product = dot_nn(turned_ref[rows, :], others[other].get()[:, start:end])
                out.ref[:, first : first + end - start] = product.astype(bf16)
            first += end - start
        for out, _ in targets:
            out.send()


def matrix_grad_call(streams, places, factors, others):
    frames, width = factors[0].shape
    inputs = [(places,)] + [(array, None) for array in (*factors, *others)]
    outs = []
    for order, pieces in streams:
        columns = sum(end - start for _, _, start, end in pieces)
        outs += [shaped((width, columns), bf16)] if order is None else [shaped((width // 2, columns), bf16)] * 2
    scratch = [pltpu.VMEM((width, frames), bf16) for _, pieces in streams for _ in pieces]
    columns = sum(end - start for _, pieces in streams for _, _, start, end in pieces)
    return staged_call(
        functools.partial(matrix_grad_kernel, streams, len(factors)), "matrix_grad", inputs, outs,
        scratch, 2 * frames * width * columns,
    )


def swap(part):
    return lax.ppermute(part, "mp", [(0, 1), (1, 0)])


def stream_order(bits, first_bits):
    order = [b for b in first_bits if b < bits] + [b for b in range(bits) if b not in first_bits]
    blocks = []
    for place in range(1 << bits):
        block = 0
        for position, bit in enumerate(order):
            if (place >> (bits - 1 - position)) & 1:
                block |= 1 << bit
        blocks.append(block)
    return order, blocks


def matrix_grads(streams, blocks, places, factors, others):
    width = factors[0].shape[1]
    shards = places.shape[1]
    piece = width // shards
    if piece % 16 == 0:
        grads = list(matrix_grad_call(streams, places, factors, others))
        return [grads.pop(0) if order is None else (grads.pop(0), grads.pop(0)) for order, _ in streams]
    results = []
    for order, pieces in streams:
        parts = []
        index = jnp.arange(shards, dtype=jnp.int32)
        if order is not None:
            index = jnp.asarray(blocks[order], jnp.int32) ^ lax.axis_index("dp")
        for factor, other, start, end in pieces:
            turned = factors[factor].T.reshape(shards, piece, -1)[index].reshape(width, -1)
            parts.append(dot_nn(turned, others[other][:, start:end]).astype(bf16))
        grad = jnp.concatenate(parts, axis=1)
        results.append(grad if order is None else (grad[width // 2 :], grad[: width // 2]))
    return results


def after(value, token):
    return lax.optimization_barrier((value, token))[0]


class Halving:
    def __init__(self, pair, order):
        self.send, self.keep = pair
        self.order = list(order)
        self.start()

    def start(self):
        bit = self.order.pop(0)
        count = lax.axis_size("dp")
        self.got = lax.ppermute(self.send, "dp", [(i, i ^ (1 << bit)) for i in range(count)])

    def step(self, token=None):
        got = self.got if token is None else after(self.got, token)
        if not self.order:
            return self.keep.astype(f32) + got.astype(f32)
        half = got.shape[0] // 2
        self.send, self.keep = (
            (self.keep[part].astype(f32) + got[part].astype(f32)).astype(bf16)
            for part in (slice(half, None), slice(0, half))
        )
        self.start()

    def finish(self):
        while self.order:
            self.step()
        return self.step()


def scattered_sum(grad):
    return lax.psum_scatter(grad, "dp", scatter_dimension=0, tiled=True).astype(f32)


def column_thirds(pieces):
    total = sum(end - start for _, _, start, end in pieces)
    third = total // 3 // LANES * LANES
    bounds = [0, third, 2 * third, total]
    streams = []
    for low, high in zip(bounds, bounds[1:]):
        place, taken = 0, []
        for factor, other, start, end in pieces:
            first, last = max(low, place), min(high, place + end - start)
            if first < last:
                taken.append((factor, other, start + first - place, start + last - place))
            place += end - start
        streams.append(tuple(taken))
    return streams


def on_device(
    frames,
    qkv_weight,
    qv_bias,
    out_weight,
    up_weight,
    up_bias,
    down_weight,
    out_bias,
    norm_gain,
    norm_shift,
    clip_lengths,
    live_lengths,
    out_grad,
):
    layer_count = qkv_weight.shape[0]
    width = qkv_weight.shape[1]
    group = qkv_weight.shape[3]
    hidden = up_weight.shape[2]
    row_count = frames.shape[0]
    shards = lax.axis_size("dp")
    bits = shards.bit_length() - 1
    piece = width // shards
    own_start = lax.axis_index("mp") * row_count
    core = lax.axis_index("mp").astype(jnp.int32)[None]
    rows_now = (frames, swap(frames), core)
    grad_other = swap(out_grad)
    qkv_parts = jnp.transpose(qkv_weight, (0, 2, 1, 3))
    norm_rows = (out_bias, norm_gain, norm_shift)
    saved = []
    for layer in range(layer_count):
        qkv, lse, mix, part, low, *norm_out = attention_forward(
            layer, clip_lengths, live_lengths, (qkv_parts, out_weight, qv_bias, norm_rows), rows_now
        )
        if layer > 0:
            saved[-1] += tuple(norm_out)
        residual = low if layer == 0 else norm_out[0]
        normed, inverse, first_low, up_value, active, ffn_part = ffn_forward(
            layer, (up_weight, down_weight, up_bias, norm_rows), (residual, part, swap(part))
        )
        rows_now = (normed, ffn_part, swap(ffn_part))
        saved.append((low, qkv, mix, lse, normed, inverse, first_low, up_value, active))
    orders, blocks = zip(*(stream_order(bits, first) for first in ([0, 1, 2], [1, 2, 0], [2, 0, 1])))
    from_own = jnp.arange(shards, dtype=jnp.int32) ^ lax.axis_index("dp").astype(jnp.int32)
    places = jnp.asarray([[order.index(block) for block in range(shards)] for order in blocks], jnp.int32)
    places = places[:, from_own]
    vector_terms = [None] * layer_count
    wide_terms = [None] * layer_count
    ffn_grads = [None] * layer_count
    attn_grads = [None] * layer_count
    running = []
    for layer in reversed(range(layer_count)):
        low, qkv, mix, lse, normed, inverse, first_low, up_value, active = saved[layer][:9]
        last = layer == layer_count - 1
        if last:
            rows = (out_grad, grad_other, *rows_now)
        else:
            rows = (*saved[layer][9:], dhidden, part, got)
        backs = ffn_backward(layer, last, (up_weight, down_weight, norm_rows), rows, up_value, core)
        dsecond, dsecond_low, dup, part, ffn_vectors, up_bias_grad = backs[:6]
        if last:
            frames_out = backs[6]
        for stream in running:
            stream.step(part)
        got = swap(part)
        ffn_pieces = ((0, 0, 0, hidden), (1, 1, 0, hidden))
        if layer > 0:
            ffn_streams = ((0, ffn_pieces[:1]), (1, ffn_pieces[1:]))
        else:
            ffn_streams = tuple(enumerate(column_thirds(ffn_pieces)))
        grads = matrix_grads(ffn_streams, blocks, places, [dsecond_low, first_low], [active, dup])
        ffn_grads[layer] = [Halving(pair, order) for pair, order in zip(grads, orders)]
        dhidden, dhidden_low, dqkv, part, attn_vectors, qv_grad = attention_backward(
            layer, clip_lengths, live_lengths, (qkv_parts, out_weight, norm_gain),
            (dsecond, part, got, normed, inverse), (qkv, mix, lse),
        )
        for stream in running:
            stream.step(part)
        running = running + ffn_grads[layer]
        got = swap(part)
        attn_pieces = ((0, 0, 0, group), (1, 1, 0, 3 * group))
        if layer > 0:
            attn_streams = ((2, attn_pieces),)
        else:
            attn_streams = tuple(enumerate(column_thirds(attn_pieces)))
        grads = matrix_grads(attn_streams, blocks, places, [dhidden_low, low], [mix, dqkv])
        attn_grads[layer] = [
            Halving(pair, orders[stream]) for pair, (stream, _) in zip(grads, attn_streams)
        ]
        running = running + attn_grads[layer]
        vector_terms[layer] = jnp.stack([attn_vectors[:3], ffn_vectors[:3]], axis=1)
        wide_terms[layer] = jnp.concatenate([qv_grad[0], qv_grad[1], up_bias_grad[0]])

    def finished(streams):
        sums = [stream.finish() if isinstance(stream, Halving) else stream for stream in streams]
        return sums[0] if len(sums) == 1 else jnp.concatenate(sums, axis=1)

    ffn_sums = [finished(streams) for streams in ffn_grads]
    attn_sums = [finished(streams) for streams in attn_grads]
    own_rows = [lax.dynamic_slice_in_dim(v, own_start, row_count, 0) for v in (dhidden, part, got)]
    input_grad = own_rows[0] + (own_rows[1].astype(f32) + own_rows[2].astype(f32))
    narrow = jnp.stack(vector_terms).reshape(layer_count * 6, shards, piece)
    narrow = jnp.transpose(narrow, (1, 0, 2)).reshape(shards, -1)
    lengths = [group, group, hidden] * layer_count
    wide_all = jnp.concatenate(wide_terms)
    wides = []
    place = 0
    for length in lengths:
        wides.append(wide_all[place : place + length].reshape(shards, length // shards))
        place += length
    small = jnp.concatenate([narrow] + wides, axis=1).astype(bf16)
    small = lax.all_to_all(small, "dp", 0, 0, tiled=True)
    small = jnp.sum(small.astype(f32), axis=0)
    vectors = small[: narrow.shape[1]].reshape(layer_count, 3, 2, piece)
    own = piece // lax.axis_size("mp")
    vectors = lax.dynamic_slice_in_dim(vectors, lax.axis_index("mp") * own, own, 3)
    wide_out = small[narrow.shape[1] :].reshape(layer_count, -1)
    q_piece = group // shards
    return (
        frames_out,
        input_grad,
        jnp.stack([g[:, group:].reshape(piece, 3, group) for g in attn_sums]),
        wide_out[:, : 2 * q_piece].reshape(layer_count, 1, 2, q_piece),
        jnp.stack([g[:, :group].T for g in attn_sums]),
        jnp.stack([g[:, hidden:] for g in ffn_sums]),
        wide_out[:, 2 * q_piece :].reshape(layer_count, 1, -1),
        jnp.stack([g[:, :hidden].T for g in ffn_sums]),
        vectors[:, 0],
        vectors[:, 1],
        vectors[:, 2],
    )


def solution(mesh):
    placed = (
        P(("dp", "mp"), None),
        P(None, None, None, "mp"),
        P(None, None, "mp"),
        P(None, "mp", None),
        P(None, None, "mp"),
        P(None, "mp"),
        P(None, "mp", None),
        P(),
        P(),
        P(),
        P("dp"),
        P("dp"),
        P(("dp", "mp"), None),
    )
    return jax.shard_map(
        on_device,
        mesh=mesh,
        in_specs=placed,
        out_specs=(
            P(("dp", "mp"), None),
            P(("dp", "mp"), None),
            P(None, "dp", None, "mp"),
            P(None, "mp", None, "dp"),
            P(None, "mp", "dp"),
            P(None, "dp", "mp"),
            P(None, "mp", "dp"),
            P(None, "mp", "dp"),
            P(None, None, ("dp", "mp")),
            P(None, None, ("dp", "mp")),
            P(None, None, ("dp", "mp")),
        ),
        check_vma=False,
    )
```
